32 devices in a mesh: seq: 16 (over z, y, core), head: 1, dp: 2 (over x).
Axes of the slice: x: 2, y: 2, z: 4, core: 2. Of those that a mesh axis runs over, the one named last changes fastest.
Arguments:
- queries: bfloat16 [22528, 2048], P(('dp', 'seq'), 'head'), parts along dimension 0, may hold values from -96 to 96
- out_grad: bfloat16 [22528, 2048], P(('dp', 'seq'), 'head'), parts along dimension 0, may hold values from -16 to 16
- encodings: bfloat16 [320, 16, 2048], P(('dp', 'seq'), None, 'head'), parts along dimension 0, may hold values from -6 to 6
- key_weight: bfloat16 [2048, 2048], P(None, 'head'), may hold values from -0.125 to 0.125
- value_weight: bfloat16 [2048, 2048], P(None, 'head'), may hold values from -0.125 to 0.125
- neighbours: int32 [352, 2], P(('dp', 'seq')), parts along dimension 0, may hold values from 0 to 159, as said below
Outputs:
- query_grad: bfloat16 [22528, 2048], P(('dp', 'seq'), 'head'), parts along dimension 0
- encoding_grad: bfloat16 [320, 16, 2048], P(('dp', 'seq'), None, 'head'), parts along dimension 0
The draws below stay inside these ranges and needn't reach their ends.
There are 2 independent parts, one for each index of `dp`. The reference program is written for one: setup_inputs(seed, part) draws one part's arguments, and reference() takes and returns one part's arrays. A program takes and returns all parts, laid end to end along the dimension named above; an argument that names none is the same for every part. Nothing has to cross between parts.
Inputs may be any that keep to these rules, and one draw needn't show every extreme that they name: `neighbours`: row r of encodings is held by index r // 10 of seq. In each aligned block of 11 spans, at most 2 of the 22 ids belong to one holder, and some holder has exactly 2. A span's two ids differ.
All inputs are finite; a program needn't handle non-finite values.
Results may differ from the reference program's by a relative error of at most 0.011.
Values may be sent and summed in bfloat16 or wider, within the bound.
A program may use at most 64 MiB of HBM per device.

```python
import math
import jax
import jax.numpy as jnp
from jax import lax

D = 2048
HEADS = 16
SPAN = 64
NBLEN = 16
TOK_DEV = 704
NB_DEV = 10
TOKENS = 11264
SPANS = 176
NROWS = 160
CAP = 2
N_SEQ = 16


def draw_queries(key, part):
    base = jnp.clip(jax.random.normal(jax.random.fold_in(key, 1), (TOKENS, D), jnp.float32), -6.0, 6.0)
    return base.astype(jnp.bfloat16)


def draw_out_grad(key, part):
    base = jnp.clip(4.0 * jax.random.normal(jax.random.fold_in(key, 2), (TOKENS, D), jnp.float32), -16.0, 16.0)
    return base.astype(jnp.bfloat16)


def draw_neighbours(key, part):
    owners_total = NROWS // NB_DEV
    spans_here = TOK_DEV // SPAN
    ref_count = 2 * spans_here
    slot_total = owners_total * CAP
    key_list = jax.random.split(key, 7)
    popular = jnp.where(jax.random.randint(key_list[0], (owners_total,), 0, 4) == 0, 4, 1).astype(jnp.int32)
    slot_owner = jnp.repeat(jnp.arange(owners_total, dtype=jnp.int32), CAP)
    favored = jax.random.randint(key_list[1], (owners_total, 1), 0, owners_total)
    raw = jax.random.randint(key_list[2], (owners_total, slot_total), 0, 4096) * popular[slot_owner][None, :]
    raw = raw + jnp.where(slot_owner[None, :] == favored, 65536, 0)
    ranked = raw * slot_total + jnp.arange(slot_total, dtype=jnp.int32)[None, :]
    _, taken = lax.top_k(ranked, ref_count)
    chosen = slot_owner[taken]
    shuffle = jax.random.randint(key_list[3], (owners_total, ref_count), 0, 65536) * ref_count + jnp.arange(ref_count, dtype=jnp.int32)[None, :]
    order = jnp.argsort(shuffle, axis=1)
    chosen = jnp.take_along_axis(chosen, order, axis=1).reshape(owners_total, spans_here, 2)
    first_row = jax.random.randint(key_list[4], (owners_total, spans_here), 0, NB_DEV)
    other_row = jax.random.randint(key_list[5], (owners_total, spans_here), 0, NB_DEV)
    offset = jax.random.randint(key_list[6], (owners_total, spans_here), 0, NB_DEV - 1)
    second_row = jnp.where(chosen[..., 0] == chosen[..., 1], (first_row + 1 + offset) % NB_DEV, other_row)
    rows_local = jnp.stack([first_row, second_row], axis=-1)
    return (chosen * NB_DEV + rows_local).reshape(SPANS, 2).astype(jnp.int32)


def steps_of(stream_key, extent, shards, smallest, top_value):
    def one(dim, shards_of):
        draws = jax.random.uniform(jax.random.fold_in(jax.random.fold_in(stream_key, 6), dim), (shards_of,), jnp.float32, smallest / len(shards), top_value / len(shards))
        return jnp.repeat(jnp.exp(draws), extent[dim] // shards_of).reshape((-1,) + (1,) * (len(extent) - dim - 1))

    gain = one(*shards[0])
    for cut in shards[1:]:
        gain = gain * one(*cut)
    return gain


def bell_draw(stream_key, extent, width, reach, pieces=(), kind=jnp.bfloat16):
    array = jax.random.normal(stream_key, extent, jnp.float32) * width
    if len(pieces) > 0:
        array = steps_of(stream_key, extent, pieces, -0.22, 0.18) * array
    return jnp.clip(array, min=-reach, max=reach).astype(kind)


def setup_inputs(seed: int = 0, part: int = 0) -> dict:
    key_of = jax.random.split(jax.random.key(seed), 7)
    part_splits = jax.random.split(jax.random.fold_in(key_of[6], part), 7)
    queries = draw_queries(jax.random.fold_in(jax.random.fold_in(key_of[6], part), 71), part)
    out_grad = draw_out_grad(jax.random.fold_in(jax.random.fold_in(key_of[6], part), 71), part)
    encodings = bell_draw(part_splits[2], (NROWS, NBLEN, D), 1.0, 6.0, ((0, 16),))
    key_weight = bell_draw(key_of[3], (D, D), D ** -0.5, 0.125)
    value_weight = bell_draw(key_of[4], (D, D), D ** -0.5, 0.125)
    neighbours = draw_neighbours(jax.random.fold_in(jax.random.fold_in(key_of[6], part), 71), part)
    return {"queries": queries, "out_grad": out_grad, "encodings": encodings, "key_weight": key_weight, "value_weight": value_weight, "neighbours": neighbours}


def round_trip(values):
    return lax.optimization_barrier(values.astype(jnp.bfloat16)).astype(jnp.float32)

def reference(queries, out_grad, encodings, key_weight, value_weight, neighbours):
    spans_here = TOK_DEV // SPAN
    ref_count = 2 * spans_here
    head_size = D // HEADS
    scaling = 1.0 / math.sqrt(head_size)
    key_full = key_weight.astype(jnp.float32)
    value_full = value_weight.astype(jnp.float32)

    def per_block(totals, block_index):
        start = block_index * TOK_DEV
        query_rows = lax.dynamic_slice_in_dim(queries, start, TOK_DEV, 0).astype(jnp.float32)
        grad_rows = lax.dynamic_slice_in_dim(out_grad, start, TOK_DEV, 0).astype(jnp.float32)
        chosen = lax.dynamic_slice_in_dim(neighbours, block_index * spans_here, spans_here, 0).reshape(ref_count).astype(jnp.int32)
        picked = jnp.take(encodings, chosen, axis=0).astype(jnp.float32)
        keys = round_trip(jnp.einsum('rld,de->rle', picked, key_full))
        values = round_trip(jnp.einsum('rld,de->rle', picked, value_full))
        query_heads = query_rows.reshape(spans_here, SPAN, HEADS, head_size)
        grad_heads = grad_rows.reshape(spans_here, SPAN, HEADS, head_size)
        key_heads = keys.reshape(spans_here, 2 * NBLEN, HEADS, head_size)
        value_heads = values.reshape(spans_here, 2 * NBLEN, HEADS, head_size)
        scores = jnp.einsum('cthd,cuhd->chtu', query_heads, key_heads) * scaling
        scores = scores - lax.optimization_barrier(jnp.max(scores, axis=-1, keepdims=True))
        raised = jnp.exp(scores)
        probs = raised / lax.optimization_barrier(jnp.sum(raised, axis=-1, keepdims=True))
        probs_b = round_trip(probs)
        attended = jnp.einsum('chtu,cuhd->cthd', probs_b, value_heads)
        delta = jnp.transpose(lax.optimization_barrier(jnp.sum(grad_heads * attended, axis=-1)), (0, 2, 1))
        dprobs = jnp.einsum('cthd,cuhd->chtu', grad_heads, value_heads)
        dscores = round_trip(probs * (dprobs - delta[..., None]))
        query_part = (jnp.einsum('chtu,cuhd->cthd', dscores, key_heads) * scaling).astype(jnp.bfloat16)
        key_grad = round_trip(jnp.einsum('chtu,cthd->cuhd', dscores, query_heads) * scaling)
        value_grad = round_trip(jnp.einsum('chtu,cthd->cuhd', probs_b, grad_heads))
        key_grad = key_grad.reshape(ref_count, NBLEN, D)
        value_grad = value_grad.reshape(ref_count, NBLEN, D)
        ref_grad = round_trip(jnp.einsum('rle,de->rld', key_grad, key_full) + jnp.einsum('rle,de->rld', value_grad, value_full))
        totals = totals.at[chosen].add(ref_grad)
        return (totals, query_part.reshape(TOK_DEV, D))
    initial = jnp.zeros((NROWS, NBLEN, D), jnp.float32)
    totals, query_parts = lax.scan(per_block, initial, jnp.arange(N_SEQ, dtype=jnp.int32))
    return (query_parts.reshape(TOKENS, D), totals.astype(jnp.bfloat16))
```

```python
import functools
import math

import jax
import jax.numpy as jnp
from jax import lax
from jax.experimental import pallas as pl
from jax.experimental.pallas import tpu as pltpu
from jax.sharding import PartitionSpec as P

D = 2048
HEADS = 16
MESH = pl.DeviceIdType.MESH
NT = (((1,), (1,)), ((), ()))
TN = (((0,), (0,)), ((), ()))
F32 = jnp.float32
BF16 = jnp.bfloat16


def one_hot(index, shape, dim):
    places = lax.broadcasted_iota(jnp.int32, shape, dim)
    return jnp.where(places == index, 1.0, 0.0).astype(BF16)


def tile(j, size):
    return pl.ds(pl.multiple_of(j * size, size), size)


def greet(n, me):
    barrier = pltpu.get_barrier_semaphore()

    def signal(k, carry):
        pl.semaphore_signal(
            barrier, inc=1, device_id={"seq": lax.rem(me + k, n)}, device_id_type=MESH
        )
        return carry

    lax.fori_loop(1, n, signal, 0)
    pl.semaphore_wait(barrier, n - 1)


def exchange(n, me, size, src, dst, send_sem, recv_sem, own_sem):
    own = pltpu.make_async_copy(src.at[tile(me, size)], dst.at[tile(me, size)], own_sem)

    def remote(k):
        peer = lax.rem(me + k, n)
        return pltpu.make_async_remote_copy(
            src_ref=src.at[tile(peer, size)],
            dst_ref=dst.at[tile(me, size)],
            send_sem=send_sem.at[k],
            recv_sem=recv_sem.at[k],
            device_id={"seq": peer},
            device_id_type=MESH,
        )

    def arrival(k):
        holder = lax.rem(me + n - k, n)
        return pltpu.make_async_remote_copy(
            src_ref=src.at[tile(holder, size)],
            dst_ref=dst.at[tile(holder, size)],
            send_sem=send_sem.at[k],
            recv_sem=recv_sem.at[k],
            device_id={"seq": holder},
            device_id_type=MESH,
        )

    def start(i, carry):
        k = lax.rem(i + n // 2 - 1, n - 1) + 1
        remote(k).start()
        return carry

    def finish(k, carry):
        arrival(k).wait_recv()
        remote(k).wait_send()
        return carry

    def start_all():
        own.start()
        lax.fori_loop(0, n - 1, start, 0)

    def wait_all():
        own.wait()
        lax.fori_loop(1, n, finish, 0)

    return start_all, wait_all


def fetch_kernel(n, want_ref, enc_ref, arrived_ref, asked_out, asked, outgoing, s1, r1, s2, r2, own):
    me = lax.axis_index("seq")
    size = want_ref.shape[0] // n
    greet(n, me)
    start, wait = exchange(n, me, size, want_ref, asked, s1, r1, own.at[0])
    start()
    wait()
    target = asked[:, 0:1]
    asked_out[...] = asked[...]
    select = one_hot(target, (asked.shape[0], enc_ref.shape[0]), 1)
    width = 512

    def column(j, carry):
        cols = tile(j, width)
        outgoing[:, cols] = jnp.dot(
            select, enc_ref[:, cols], preferred_element_type=F32
        ).astype(BF16)
        return carry

    lax.fori_loop(0, enc_ref.shape[1] // width, column, 0)
    start, wait = exchange(n, me, size, outgoing, arrived_ref, s2, r2, own.at[1])
    start()
    wait()


def give_back_kernel(n, asked_ref, returning_ref, grad_ref, came, s1, r1, own):
    me = lax.axis_index("seq")
    size = asked_ref.shape[0] // n
    greet(n, me)
    start, wait = exchange(n, me, size, returning_ref, came, s1, r1, own.at[0])
    start()
    select = one_hot(asked_ref[:, 0:1], (asked_ref.shape[0], grad_ref.shape[0]), 1)
    wait()
    width = 512

    def column(j, carry):
        cols = tile(j, width)
        grad_ref[:, cols] = lax.dot_general(
            select, came[:, cols], TN, preferred_element_type=F32
        ).astype(BF16)
        return carry

    lax.fori_loop(0, grad_ref.shape[1] // width, column, 0)


def reader_kernel(
    spans, place_ref, place_row, arr_hbm, q_hbm, g_hbm, wk_hbm, wv_hbm, qg_hbm, ret_hbm,
    arr, q, g, wk, wv, qg, picked, keys, vals, kg, vg, ret, sem, wsem, osem,
):
    width = 256
    parts = 4
    wide = wk.shape[1] // parts
    head = D // HEADS
    span = q.shape[0] // spans
    pair = keys.shape[0] // spans
    scaling = 1.0 / math.sqrt(head)
    first = pltpu.make_async_copy(arr_hbm, arr, sem.at[0])
    first.start()
    weights = []
    for j in range(parts):
        cols = pl.ds(j * wide, wide)
        both = [
            pltpu.make_async_copy(h.at[:, cols], v.at[:, cols], wsem.at[i, j])
            for i, (h, v) in enumerate(((wk_hbm, wk), (wv_hbm, wv)))
        ]
        for copy in both:
            copy.start()
        weights.append(both)
    loads = [
        pltpu.make_async_copy(q_hbm, q, sem.at[1]),
        pltpu.make_async_copy(g_hbm, g, sem.at[2]),
    ]
    for copy in loads:
        copy.start()
    count, slots = keys.shape[0], arr.shape[0]
    first.wait()
    gather = one_hot(place_ref[:, 0:1], (count, slots), 1)

    def pick(j, carry):
        cols = tile(j, width)
        picked[:, cols] = jnp.dot(gather, arr[:, cols], preferred_element_type=F32).astype(BF16)
        return carry

    lax.fori_loop(0, D // width, pick, 0)

    def project(j, carry):
        cols = tile(j, width)
        keys[:, cols] = jnp.dot(picked[...], wk[:, cols], preferred_element_type=F32).astype(BF16)
        vals[:, cols] = jnp.dot(picked[...], wv[:, cols], preferred_element_type=F32).astype(BF16)
        return carry

    for j in range(parts):
        for copy in weights[j]:
            copy.wait()
        lax.fori_loop(j * wide // width, (j + 1) * wide // width, project, 0)
    for copy in loads:
        copy.wait()

    def attend(c, carry):
        toks, nbrs = tile(c, span), tile(c, pair)
        for h in range(HEADS):
            cols = slice(h * head, (h + 1) * head)
            qh, gh = q[toks, cols], g[toks, cols]
            kh, vh = keys[nbrs, cols], vals[nbrs, cols]
            scores = lax.dot_general(kh, qh, NT, preferred_element_type=F32) * scaling
            raised = jnp.exp(scores - jnp.max(scores, axis=0, keepdims=True))
            probs = raised / jnp.sum(raised, axis=0, keepdims=True)
            probs_b = probs.astype(BF16)
            dprobs = lax.dot_general(vh, gh, NT, preferred_element_type=F32)
            delta = jnp.sum(probs_b.astype(F32) * dprobs, axis=0, keepdims=True)
            dscores = (probs * (dprobs - delta)).astype(BF16)
            dq = lax.dot_general(dscores, kh, TN, preferred_element_type=F32) * scaling
            qg[toks, cols] = dq.astype(BF16)
            dk = jnp.dot(dscores, qh, preferred_element_type=F32) * scaling
            kg[nbrs, cols] = dk.astype(BF16)
            vg[nbrs, cols] = jnp.dot(probs_b, gh, preferred_element_type=F32).astype(BF16)
        pltpu.make_async_copy(qg.at[toks], qg_hbm.at[toks], osem.at[c]).start()
        return carry

    lax.fori_loop(0, spans, attend, 0)
    spread = one_hot(place_row[0:1, :], (slots, count), 0)

    def back(j, carry):
        cols = tile(j, width)
        total = lax.dot_general(kg[...], wk[cols, :], NT, preferred_element_type=F32)
        total = total + lax.dot_general(vg[...], wv[cols, :], NT, preferred_element_type=F32)
        ret[:, cols] = jnp.dot(
            spread, total.astype(BF16), preferred_element_type=F32
        ).astype(BF16)
        return carry

    lax.fori_loop(0, D // width, back, 0)
    done = pltpu.make_async_copy(ret, ret_hbm, sem.at[3])
    done.start()

    def landed(c, carry):
        toks = tile(c, span)
        pltpu.make_async_copy(qg.at[toks], qg_hbm.at[toks], osem.at[c]).wait()
        return carry

    lax.fori_loop(0, spans, landed, 0)
    done.wait()


def on_device_whole_heads(queries, out_grad, encodings, key_weight, value_weight, neighbours):
    n = lax.axis_size("seq")
    spans = neighbours.shape[0]
    refs = 2 * spans
    rows, length, width = encodings.shape
    toks = queries.shape[0]
    capacity = max(2, refs // n)
    slots = n * capacity
    ids = neighbours.reshape(refs)
    owner = ids // rows
    place = owner * capacity + slot_ranks(owner)
    hit = place[None, :] == jnp.arange(slots, dtype=jnp.int32)[:, None]
    row = jnp.max(jnp.where(hit, (ids % rows)[None, :], -1), axis=1)
    token = jnp.arange(length, dtype=jnp.int32)
    want = jnp.where(row[:, None] >= 0, row[:, None] * length + token[None, :], -1)
    want = jnp.broadcast_to(want.reshape(slots * length, 1), (slots * length, 128))
    place = (place[:, None] * length + token[None, :]).reshape(refs * length)
    place_col = jnp.broadcast_to(place[:, None], (refs * length, 128))
    place_row = jnp.broadcast_to(place[None, :], (8, refs * length))
    vmem = pl.BlockSpec(memory_space=pltpu.VMEM)
    hbm = pl.BlockSpec(memory_space=pl.ANY)
    dma = pltpu.SemaphoreType.DMA
    total = slots * length
    arrived, asked = pl.pallas_call(
        functools.partial(fetch_kernel, n),
        out_shape=(
            jax.ShapeDtypeStruct((total, width), BF16),
            jax.ShapeDtypeStruct((total, 128), jnp.int32),
        ),
        in_specs=[vmem, vmem],
        out_specs=(hbm, vmem),
        scratch_shapes=[
            pltpu.VMEM((total, 128), jnp.int32),
            pltpu.VMEM((total, width), BF16),
            dma((n,)), dma((n,)), dma((n,)), dma((n,)), dma((2,)),
        ],
        compiler_params=pltpu.CompilerParams(
            collective_id=0, has_side_effects=True, vmem_limit_bytes=16 << 20
        ),
    )(want, encodings.reshape(rows * length, width))
    count = refs * length
    query_grad, returning = pl.pallas_call(
        functools.partial(reader_kernel, spans),
        out_shape=(
            jax.ShapeDtypeStruct((toks, width), BF16),
            jax.ShapeDtypeStruct((total, width), BF16),
        ),
        in_specs=[vmem, vmem, hbm, hbm, hbm, hbm, hbm],
        out_specs=(hbm, hbm),
        scratch_shapes=[
            pltpu.VMEM((total, width), BF16),
            pltpu.VMEM((toks, width), BF16),
            pltpu.VMEM((toks, width), BF16),
            pltpu.VMEM((width, width), BF16),
            pltpu.VMEM((width, width), BF16),
            pltpu.VMEM((toks, width), BF16),
            pltpu.VMEM((count, width), BF16),
            pltpu.VMEM((count, width), BF16),
            pltpu.VMEM((count, width), BF16),
            pltpu.VMEM((count, width), BF16),
            pltpu.VMEM((count, width), BF16),
            pltpu.VMEM((total, width), BF16),
            dma((4,)), dma((2, 4)), dma((spans,)),
        ],
        compiler_params=pltpu.CompilerParams(vmem_limit_bytes=56 << 20),
    )(place_col, place_row, arrived, queries, out_grad, key_weight, value_weight)
    encoding_grad = pl.pallas_call(
        functools.partial(give_back_kernel, n),
        out_shape=jax.ShapeDtypeStruct((rows * length, width), BF16),
        in_specs=[vmem, hbm],
        out_specs=vmem,
        scratch_shapes=[
            pltpu.VMEM((total, width), BF16),
            dma((n,)), dma((n,)), dma((2,)),
        ],
        compiler_params=pltpu.CompilerParams(
            collective_id=1, has_side_effects=True, vmem_limit_bytes=16 << 20
        ),
    )(asked, returning)
    return query_grad, encoding_grad.reshape(rows, length, width)


def slot_ranks(owner_ids):
    count = owner_ids.shape[-1]
    same_owner = owner_ids[..., :, None] == owner_ids[..., None, :]
    positions = jnp.arange(count, dtype=jnp.int32)
    earlier = positions[None, :] < positions[:, None]
    return jnp.sum(same_owner & earlier, axis=-1)


def on_device(queries, out_grad, encodings, key_weight, value_weight, neighbours):
    seq_count = lax.axis_size("seq")
    seq_index = lax.axis_index("seq")
    spans_here = neighbours.shape[0]
    ref_count = 2 * spans_here
    rows_here, neighbour_len, half_width = encodings.shape
    full_width = key_weight.shape[0]
    tok_rows = queries.shape[0]
    span_len = tok_rows // spans_here
    head_size = D // HEADS
    heads_here = half_width // head_size
    scaling = 1.0 / math.sqrt(head_size)
    capacity = max(2, ref_count // seq_count)
    slot_count = seq_count * capacity
    all_lists = lax.all_gather(neighbours, "seq", axis=0, tiled=True).reshape(seq_count, ref_count)
    owner_table = all_lists // rows_here
    local_table = all_lists % rows_here
    rank_table = slot_ranks(owner_table)
    own_ids = neighbours.reshape(ref_count)
    own_owner = own_ids // rows_here
    position = own_owner * capacity + slot_ranks(own_owner)
    slot_ids = jnp.arange(capacity, dtype=jnp.int32)
    chosen = (owner_table == seq_index)[:, None, :] & (
        rank_table[:, None, :] == slot_ids[None, :, None]
    )
    filled = jnp.any(chosen, axis=-1)
    slot_row = jnp.sum(jnp.where(chosen, local_table[:, None, :], 0), axis=-1)
    select = filled[..., None] & (
        slot_row[..., None] == jnp.arange(rows_here, dtype=jnp.int32)[None, None, :]
    )
    select = select.astype(jnp.bfloat16).reshape(slot_count, rows_here)
    flat_enc = encodings.reshape(rows_here, neighbour_len * half_width)
    outgoing = jnp.dot(select, flat_enc, preferred_element_type=jnp.float32).astype(jnp.bfloat16)
    outgoing = outgoing.reshape(seq_count, capacity, neighbour_len, half_width)
    arrived = lax.all_to_all(outgoing, "seq", split_axis=0, concat_axis=0, tiled=True)
    flat_arrived = arrived.reshape(slot_count, neighbour_len, half_width)
    whole = lax.all_gather(flat_arrived, "head", axis=2, tiled=True)
    pick = (position[:, None] == jnp.arange(slot_count, dtype=jnp.int32)[None, :]).astype(
        jnp.bfloat16
    )
    full_rows = jnp.dot(
        pick, whole.reshape(slot_count, neighbour_len * full_width),
        preferred_element_type=jnp.float32,
    ).astype(jnp.bfloat16)
    flat_rows = full_rows.reshape(ref_count * neighbour_len, full_width)
    keys = jnp.dot(flat_rows, key_weight, preferred_element_type=jnp.float32).astype(jnp.bfloat16)
    values = jnp.dot(flat_rows, value_weight, preferred_element_type=jnp.float32).astype(
        jnp.bfloat16
    )
    query_heads = queries.reshape(spans_here, span_len, heads_here, head_size)
    grad_heads = out_grad.reshape(spans_here, span_len, heads_here, head_size)
    key_heads = keys.reshape(spans_here, 2 * neighbour_len, heads_here, head_size)
    value_heads = values.reshape(spans_here, 2 * neighbour_len, heads_here, head_size)
    scores = (
        jnp.einsum("cthd,cuhd->chtu", query_heads, key_heads, preferred_element_type=jnp.float32)
        * scaling
    )
    scores = scores - jnp.max(scores, axis=-1, keepdims=True)
    raised = jnp.exp(scores)
    probs = raised / jnp.sum(raised, axis=-1, keepdims=True)
    probs_b = probs.astype(jnp.bfloat16)
    attended = jnp.einsum(
        "chtu,cuhd->cthd", probs_b, value_heads, preferred_element_type=jnp.float32
    )
    delta = jnp.transpose(jnp.sum(grad_heads.astype(jnp.float32) * attended, axis=-1), (0, 2, 1))
    dprobs = jnp.einsum(
        "cthd,cuhd->chtu", grad_heads, value_heads, preferred_element_type=jnp.float32
    )
    dscores = (probs * (dprobs - delta[..., None])).astype(jnp.bfloat16)
    query_grad = (
        jnp.einsum("chtu,cuhd->cthd", dscores, key_heads, preferred_element_type=jnp.float32)
        * scaling
    )
    query_grad = query_grad.astype(jnp.bfloat16).reshape(tok_rows, half_width)
    key_grad = (
        jnp.einsum("chtu,cthd->cuhd", dscores, query_heads, preferred_element_type=jnp.float32)
        * scaling
    )
    key_grad = key_grad.astype(jnp.bfloat16).reshape(ref_count * neighbour_len, half_width)
    value_grad = jnp.einsum(
        "chtu,cthd->cuhd", probs_b, grad_heads, preferred_element_type=jnp.float32
    )
    value_grad = value_grad.astype(jnp.bfloat16).reshape(ref_count * neighbour_len, half_width)
    contract = (((1,), (1,)), ((), ()))
    partial_value = lax.dot_general(
        key_grad, key_weight, contract, preferred_element_type=jnp.float32
    )
    partial_value = partial_value + lax.dot_general(
        value_grad, value_weight, contract, preferred_element_type=jnp.float32
    )
    summed = lax.psum_scatter(
        partial_value.reshape(ref_count, neighbour_len, full_width),
        "head",
        scatter_dimension=2,
        tiled=True,
    )
    ref_grad = summed.astype(jnp.bfloat16)
    returning = (
        jnp.zeros((slot_count, neighbour_len, half_width), jnp.bfloat16).at[position].set(ref_grad)
    )
    returning = returning.reshape(seq_count, capacity, neighbour_len, half_width)
    came_back = lax.all_to_all(returning, "seq", split_axis=0, concat_axis=0, tiled=True).reshape(
        slot_count, neighbour_len * half_width
    )
    encoding_grad = lax.dot_general(
        select, came_back, (((0,), (0,)), ((), ())), preferred_element_type=jnp.float32
    )
    encoding_grad = encoding_grad.astype(jnp.bfloat16).reshape(rows_here, neighbour_len, half_width)
    return (query_grad, encoding_grad)


def solution(mesh):
    body = on_device_whole_heads if mesh.shape["head"] == 1 else on_device
    return jax.shard_map(
        body,
        mesh=mesh,
        in_specs=(
            P(("dp", "seq"), "head"),
            P(("dp", "seq"), "head"),
            P(("dp", "seq"), None, "head"),
            P(None, "head"),
            P(None, "head"),
            P(("dp", "seq"), None),
        ),
        out_specs=(P(("dp", "seq"), "head"), P(("dp", "seq"), None, "head")),
        check_vma=False,
    )
```

```python
import functools
import math

import jax
import jax.numpy as jnp
from jax import lax
from jax.experimental import pallas as pl
from jax.experimental.pallas import tpu as pltpu
from jax.sharding import PartitionSpec as P

D = 2048
HEADS = 16
MESH = pl.DeviceIdType.MESH
NT = (((1,), (1,)), ((), ()))
TN = (((0,), (0,)), ((), ()))
F32 = jnp.float32
BF16 = jnp.bfloat16


def one_hot(index, shape, dim):
    places = lax.broadcasted_iota(jnp.int32, shape, dim)
    return jnp.where(places == index, 1.0, 0.0).astype(BF16)


def tile(j, size):
    return pl.ds(pl.multiple_of(j * size, size), size)


def greet(n, me):
    barrier = pltpu.get_barrier_semaphore()

    def signal(k, carry):
        pl.semaphore_signal(
            barrier, inc=1, device_id={"seq": lax.rem(me + k, n)}, device_id_type=MESH
        )
        return carry

    lax.fori_loop(1, n, signal, 0)
    pl.semaphore_wait(barrier, n - 1)


def exchange(n, me, size, src, dst, cols, send_sem, recv_sem, own_sem):
    def block(ref, p):
        return ref.at[tile(p, size), cols]

    own = pltpu.make_async_copy(block(src, me), block(dst, me), own_sem)

    def remote(k):
        peer = lax.rem(me + k, n)
        return pltpu.make_async_remote_copy(
            src_ref=block(src, peer),
            dst_ref=block(dst, me),
            send_sem=send_sem.at[k],
            recv_sem=recv_sem.at[k],
            device_id={"seq": peer},
            device_id_type=MESH,
        )

    def arrival(k):
        holder = lax.rem(me + n - k, n)
        return pltpu.make_async_remote_copy(
            src_ref=block(src, holder),
            dst_ref=block(dst, holder),
            send_sem=send_sem.at[k],
            recv_sem=recv_sem.at[k],
            device_id={"seq": holder},
            device_id_type=MESH,
        )

    def start(i, carry):
        remote(lax.rem(i + n // 2 - 1, n - 1) + 1).start()
        return carry

    def received(k, carry):
        arrival(k).wait_recv()
        return carry

    def sent(k, carry):
        remote(k).wait_send()
        return carry

    def start_all():
        own.start()
        lax.fori_loop(0, n - 1, start, 0)

    def wait_received():
        own.wait()
        lax.fori_loop(1, n, received, 0)

    def wait_sent():
        lax.fori_loop(1, n, sent, 0)

    return start_all, wait_received, wait_sent


def kernel(
    n, spans, want_ref, place_ref, place_row, enc_ref, q_hbm, g_hbm, wk_hbm, wv_hbm,
    qg_hbm, grad_ref,
    asked, outgoing, arr, q, g, wk, wv, qg, key_sum, val_sum, keys, vals, kg, vg, ret, came,
    sem, wsem, own, ids_s, ids_r, out_s, out_r, back_s, back_r,
):
    me = lax.axis_index("seq")
    parts = own.shape[1]
    wide = enc_ref.shape[1] // parts
    width = 256
    head = D // HEADS
    span = q.shape[0] // spans
    pair = keys.shape[0] // spans
    size = want_ref.shape[0] // n
    count, slots, held = keys.shape[0], arr.shape[0], enc_ref.shape[0]
    scaling = 1.0 / math.sqrt(head)

    weights = []
    for j in range(parts):
        rows = pl.ds(j * wide, wide)
        both = [
            pltpu.make_async_copy(h.at[rows], v.at[rows], wsem.at[i, j])
            for i, (h, v) in enumerate(((wk_hbm, wk), (wv_hbm, wv)))
        ]
        for copy in both:
            copy.start()
        weights.append(both)
    loads = [
        pltpu.make_async_copy(q_hbm, q, sem.at[0]),
        pltpu.make_async_copy(g_hbm, g, sem.at[1]),
    ]
    for copy in loads:
        copy.start()

    greet(n, me)
    start, received, sent = exchange(
        n, me, size, want_ref, asked, slice(None), ids_s, ids_r, sem.at[2]
    )
    start()
    received()
    sent()
    select = one_hot(asked[:, 0:1], (slots, held), 1)

    def fetch(j):
        return exchange(
            n, me, size, outgoing, arr, tile(j, wide), out_s.at[j], out_r.at[j], own.at[0, j]
        )

    def serve(j, carry):
        cols = tile(j, wide)
        outgoing[:, cols] = jnp.dot(
            select, enc_ref[:, cols], preferred_element_type=F32
        ).astype(BF16)
        fetch(j)[0]()
        return carry

    lax.fori_loop(0, parts, serve, 0)

    gather = one_hot(place_ref[:, 0:1], (count, slots), 1)
    for j in range(parts):
        for copy in weights[j]:
            copy.wait()
        fetch(j)[1]()
        deep = slice(j * wide, (j + 1) * wide)
        picked = jnp.dot(gather, arr[:, deep], preferred_element_type=F32).astype(BF16)

        def project(i, carry):
            cols = tile(i, width)
            for w, total, result in ((wk, key_sum, keys), (wv, val_sum, vals)):
                part = jnp.dot(picked, w[deep, cols], preferred_element_type=F32)
                if j > 0:
                    part = part + total[:, cols]
                if j < parts - 1:
                    total[:, cols] = part
                else:
                    result[:, cols] = part.astype(BF16)
            return carry

        lax.fori_loop(0, D // width, project, 0)
    for copy in loads:
        copy.wait()

    def attend(c, together):
        toks = pl.ds(pl.multiple_of(c * span, span), together * span)
        nbrs = pl.ds(pl.multiple_of(c * pair, pair), together * pair)
        rows, lanes = 2 * together * pair, together * span
        own = lax.rem(lax.broadcasted_iota(jnp.int32, (rows, lanes), 0) // pair, together)
        mine = own == lax.broadcasted_iota(jnp.int32, (rows, lanes), 1) // span
        gap = jnp.zeros((together * pair, head), BF16)

        def apart(two):
            upper = jnp.concatenate([two[:, :head], gap], axis=1)
            return jnp.concatenate([upper, jnp.concatenate([gap, two[:, head:]], axis=1)], axis=0)

        for h in range(0, HEADS, 2):
            cols = slice(h * head, (h + 2) * head)
            one, two = slice(h * head, (h + 1) * head), slice((h + 1) * head, (h + 2) * head)
            half = together * pair
            qh, gh = q[toks, cols], g[toks, cols]
            kh, vh = apart(keys[nbrs, cols]), apart(vals[nbrs, cols])
            scores = lax.dot_general(kh, qh, NT, preferred_element_type=F32) * scaling
            scores = jnp.where(mine, scores, -jnp.inf).reshape(2, half, lanes)
            raised = jnp.exp(scores - jnp.max(scores, axis=1, keepdims=True))
            probs = raised * (1.0 / jnp.sum(raised, axis=1, keepdims=True))
            probs_b = probs.astype(BF16)
            dprobs = lax.dot_general(vh, gh, NT, preferred_element_type=F32)
            dprobs = dprobs.reshape(2, half, lanes)
            delta = jnp.sum(probs_b.astype(F32) * dprobs, axis=1, keepdims=True)
            dscores = (probs * (dprobs - delta)).astype(BF16).reshape(rows, lanes)
            dq = lax.dot_general(dscores, kh, TN, preferred_element_type=F32) * scaling
            qg[toks, cols] = dq.astype(BF16)
            dk = jnp.dot(dscores, qh, preferred_element_type=F32)
            kg[nbrs, one] = (dk[:half, :head] * scaling).astype(BF16)
            kg[nbrs, two] = (dk[half:, head:] * scaling).astype(BF16)
            dv = jnp.dot(probs_b.reshape(rows, lanes), gh, preferred_element_type=F32)
            vg[nbrs, one] = dv[:half, :head].astype(BF16)
            vg[nbrs, two] = dv[half:, head:].astype(BF16)

    def attend_two(i, carry):
        attend(i * 2, 2)
        return carry

    lax.fori_loop(0, spans // 2, attend_two, 0)
    if spans % 2:
        attend(spans - 1, 1)
    query_done = pltpu.make_async_copy(qg, qg_hbm, sem.at[3])
    query_done.start()
    spread = one_hot(place_row[0:1, :], (slots, count), 0)

    def give_back(j):
        return exchange(
            n, me, size, ret, came, tile(j, wide), back_s.at[j], back_r.at[j], own.at[1, j]
        )

    def back(j, carry):
        cols = tile(j, wide)
        total = lax.dot_general(kg[...], wk[cols, :], NT, preferred_element_type=F32)
        total = total + lax.dot_general(vg[...], wv[cols, :], NT, preferred_element_type=F32)
        ret[:, cols] = jnp.dot(
            spread, total.astype(BF16), preferred_element_type=F32
        ).astype(BF16)
        give_back(j)[0]()
        return carry

    lax.fori_loop(0, parts, back, 0)

    def finish(j, carry):
        give_back(j)[1]()
        cols = tile(j, wide)
        grad_ref[:, cols] = lax.dot_general(
            select, came[:, cols], TN, preferred_element_type=F32
        ).astype(BF16)
        fetch(j)[2]()
        give_back(j)[2]()
        return carry

    lax.fori_loop(0, parts, finish, 0)
    query_done.wait()


def on_device_whole_heads(queries, out_grad, encodings, key_weight, value_weight, neighbours):
    n = lax.axis_size("seq")
    spans = neighbours.shape[0]
    refs = 2 * spans
    rows, length, width = encodings.shape
    toks = queries.shape[0]
    capacity = max(2, refs // n)
    slots = n * capacity
    ids = neighbours.reshape(refs)
    owner = ids // rows
    place = owner * capacity + slot_ranks(owner)
    hit = place[None, :] == jnp.arange(slots, dtype=jnp.int32)[:, None]
    row = jnp.max(jnp.where(hit, (ids % rows)[None, :], -1), axis=1)
    token = jnp.arange(length, dtype=jnp.int32)
    want = jnp.where(row[:, None] >= 0, row[:, None] * length + token[None, :], -1)
    want = jnp.broadcast_to(want.reshape(slots * length, 1), (slots * length, 128))
    place = (place[:, None] * length + token[None, :]).reshape(refs * length)
    place_col = jnp.broadcast_to(place[:, None], (refs * length, 128))
    place_row = jnp.broadcast_to(place[None, :], (8, refs * length))
    vmem = pl.BlockSpec(memory_space=pltpu.VMEM)
    hbm = pl.BlockSpec(memory_space=pl.ANY)
    dma = pltpu.SemaphoreType.DMA
    total = slots * length
    count = refs * length
    parts = 4
    query_grad, encoding_grad = pl.pallas_call(
        functools.partial(kernel, n, spans),
        out_shape=(
            jax.ShapeDtypeStruct((toks, width), BF16),
            jax.ShapeDtypeStruct((rows * length, width), BF16),
        ),
        in_specs=[vmem, vmem, vmem, vmem, hbm, hbm, hbm, hbm],
        out_specs=(hbm, vmem),
        scratch_shapes=[
            pltpu.VMEM((total, 128), jnp.int32),
            pltpu.VMEM((total, width), BF16),
            pltpu.VMEM((total, width), BF16),
            pltpu.VMEM((toks, width), BF16),
            pltpu.VMEM((toks, width), BF16),
            pltpu.VMEM((width, width), BF16),
            pltpu.VMEM((width, width), BF16),
            pltpu.VMEM((toks, width), BF16),
            pltpu.VMEM((count, width), F32),
            pltpu.VMEM((count, width), F32),
            pltpu.VMEM((count, width), BF16),
            pltpu.VMEM((count, width), BF16),
            pltpu.VMEM((count, width), BF16),
            pltpu.VMEM((count, width), BF16),
            pltpu.VMEM((total, width), BF16),
            pltpu.VMEM((total, width), BF16),
            dma((4,)), dma((2, parts)), dma((2, parts)),
            dma((n,)), dma((n,)),
            dma((parts, n)), dma((parts, n)), dma((parts, n)), dma((parts, n)),
        ],
        compiler_params=pltpu.CompilerParams(
            collective_id=0, has_side_effects=True, vmem_limit_bytes=58 << 20
        ),
    )(
        want, place_col, place_row, encodings.reshape(rows * length, width),
        queries, out_grad, key_weight, value_weight,
    )
    return query_grad, encoding_grad.reshape(rows, length, width)


def slot_ranks(owner_ids):
    count = owner_ids.shape[-1]
    same_owner = owner_ids[..., :, None] == owner_ids[..., None, :]
    positions = jnp.arange(count, dtype=jnp.int32)
    earlier = positions[None, :] < positions[:, None]
    return jnp.sum(same_owner & earlier, axis=-1)


def on_device(queries, out_grad, encodings, key_weight, value_weight, neighbours):
    seq_count = lax.axis_size("seq")
    seq_index = lax.axis_index("seq")
    spans_here = neighbours.shape[0]
    ref_count = 2 * spans_here
    rows_here, neighbour_len, half_width = encodings.shape
    full_width = key_weight.shape[0]
    tok_rows = queries.shape[0]
    span_len = tok_rows // spans_here
    head_size = D // HEADS
    heads_here = half_width // head_size
    scaling = 1.0 / math.sqrt(head_size)
    capacity = max(2, ref_count // seq_count)
    slot_count = seq_count * capacity
    all_lists = lax.all_gather(neighbours, "seq", axis=0, tiled=True).reshape(seq_count, ref_count)
    owner_table = all_lists // rows_here
    local_table = all_lists % rows_here
    rank_table = slot_ranks(owner_table)
    own_ids = neighbours.reshape(ref_count)
    own_owner = own_ids // rows_here
    position = own_owner * capacity + slot_ranks(own_owner)
    slot_ids = jnp.arange(capacity, dtype=jnp.int32)
    chosen = (owner_table == seq_index)[:, None, :] & (
        rank_table[:, None, :] == slot_ids[None, :, None]
    )
    filled = jnp.any(chosen, axis=-1)
    slot_row = jnp.sum(jnp.where(chosen, local_table[:, None, :], 0), axis=-1)
    select = filled[..., None] & (
        slot_row[..., None] == jnp.arange(rows_here, dtype=jnp.int32)[None, None, :]
    )
    select = select.astype(jnp.bfloat16).reshape(slot_count, rows_here)
    flat_enc = encodings.reshape(rows_here, neighbour_len * half_width)
    outgoing = jnp.dot(select, flat_enc, preferred_element_type=jnp.float32).astype(jnp.bfloat16)
    outgoing = outgoing.reshape(seq_count, capacity, neighbour_len, half_width)
    arrived = lax.all_to_all(outgoing, "seq", split_axis=0, concat_axis=0, tiled=True)
    flat_arrived = arrived.reshape(slot_count, neighbour_len, half_width)
    whole = lax.all_gather(flat_arrived, "head", axis=2, tiled=True)
    pick = (position[:, None] == jnp.arange(slot_count, dtype=jnp.int32)[None, :]).astype(
        jnp.bfloat16
    )
    full_rows = jnp.dot(
        pick, whole.reshape(slot_count, neighbour_len * full_width),
        preferred_element_type=jnp.float32,
    ).astype(jnp.bfloat16)
    flat_rows = full_rows.reshape(ref_count * neighbour_len, full_width)
    keys = jnp.dot(flat_rows, key_weight, preferred_element_type=jnp.float32).astype(jnp.bfloat16)
    values = jnp.dot(flat_rows, value_weight, preferred_element_type=jnp.float32).astype(
        jnp.bfloat16
    )
    query_heads = queries.reshape(spans_here, span_len, heads_here, head_size)
    grad_heads = out_grad.reshape(spans_here, span_len, heads_here, head_size)
    key_heads = keys.reshape(spans_here, 2 * neighbour_len, heads_here, head_size)
    value_heads = values.reshape(spans_here, 2 * neighbour_len, heads_here, head_size)
    scores = (
        jnp.einsum("cthd,cuhd->chtu", query_heads, key_heads, preferred_element_type=jnp.float32)
        * scaling
    )
    scores = scores - jnp.max(scores, axis=-1, keepdims=True)
    raised = jnp.exp(scores)
    probs = raised / jnp.sum(raised, axis=-1, keepdims=True)
    probs_b = probs.astype(jnp.bfloat16)
    attended = jnp.einsum(
        "chtu,cuhd->cthd", probs_b, value_heads, preferred_element_type=jnp.float32
    )
    delta = jnp.transpose(jnp.sum(grad_heads.astype(jnp.float32) * attended, axis=-1), (0, 2, 1))
    dprobs = jnp.einsum(
        "cthd,cuhd->chtu", grad_heads, value_heads, preferred_element_type=jnp.float32
    )
    dscores = (probs * (dprobs - delta[..., None])).astype(jnp.bfloat16)
    query_grad = (
        jnp.einsum("chtu,cuhd->cthd", dscores, key_heads, preferred_element_type=jnp.float32)
        * scaling
    )
    query_grad = query_grad.astype(jnp.bfloat16).reshape(tok_rows, half_width)
    key_grad = (
        jnp.einsum("chtu,cthd->cuhd", dscores, query_heads, preferred_element_type=jnp.float32)
        * scaling
    )
    key_grad = key_grad.astype(jnp.bfloat16).reshape(ref_count * neighbour_len, half_width)
    value_grad = jnp.einsum(
        "chtu,cthd->cuhd", probs_b, grad_heads, preferred_element_type=jnp.float32
    )
    value_grad = value_grad.astype(jnp.bfloat16).reshape(ref_count * neighbour_len, half_width)
    contract = (((1,), (1,)), ((), ()))
    partial_value = lax.dot_general(
        key_grad, key_weight, contract, preferred_element_type=jnp.float32
    )
    partial_value = partial_value + lax.dot_general(
        value_grad, value_weight, contract, preferred_element_type=jnp.float32
    )
    summed = lax.psum_scatter(
        partial_value.reshape(ref_count, neighbour_len, full_width),
        "head",
        scatter_dimension=2,
        tiled=True,
    )
    ref_grad = summed.astype(jnp.bfloat16)
    returning = (
        jnp.zeros((slot_count, neighbour_len, half_width), jnp.bfloat16).at[position].set(ref_grad)
    )
    returning = returning.reshape(seq_count, capacity, neighbour_len, half_width)
    came_back = lax.all_to_all(returning, "seq", split_axis=0, concat_axis=0, tiled=True).reshape(
        slot_count, neighbour_len * half_width
    )
    encoding_grad = lax.dot_general(
        select, came_back, (((0,), (0,)), ((), ())), preferred_element_type=jnp.float32
    )
    encoding_grad = encoding_grad.astype(jnp.bfloat16).reshape(rows_here, neighbour_len, half_width)
    return (query_grad, encoding_grad)


def solution(mesh):
    body = on_device_whole_heads if mesh.shape["head"] == 1 else on_device
    return jax.shard_map(
        body,
        mesh=mesh,
        in_specs=(
            P(("dp", "seq"), "head"),
            P(("dp", "seq"), "head"),
            P(("dp", "seq"), None, "head"),
            P(None, "head"),
            P(None, "head"),
            P(("dp", "seq"), None),
        ),
        out_specs=(P(("dp", "seq"), "head"), P(("dp", "seq"), None, "head")),
        check_vma=False,
    )
```

```python
import functools
import math

import jax
import jax.numpy as jnp
from jax import lax
from jax.experimental import pallas as pl
from jax.experimental.pallas import tpu as pltpu
from jax.sharding import PartitionSpec as P

D = 2048
HEADS = 16
MESH = pl.DeviceIdType.MESH
NT = (((1,), (1,)), ((), ()))
TN = (((0,), (0,)), ((), ()))
F32 = jnp.float32
BF16 = jnp.bfloat16


def one_hot(index, shape, dim):
    places = lax.broadcasted_iota(jnp.int32, shape, dim)
    return jnp.where(places == index, 1.0, 0.0).astype(BF16)


def tile(j, size):
    return pl.ds(pl.multiple_of(j * size, size), size)


def greet(n, me):
    barrier = pltpu.get_barrier_semaphore()

    def signal(k, carry):
        pl.semaphore_signal(
            barrier, inc=1, device_id={"seq": lax.rem(me + k, n)}, device_id_type=MESH
        )
        return carry

    lax.fori_loop(1, n, signal, 0)
    pl.semaphore_wait(barrier, n - 1)


def exchange(n, me, size, src, dst, cols, send_sem, recv_sem, own_sem):
    def block(ref, p):
        return ref.at[tile(p, size), cols]

    own = pltpu.make_async_copy(block(src, me), block(dst, me), own_sem)

    def remote(k):
        peer = lax.rem(me + k, n)
        return pltpu.make_async_remote_copy(
            src_ref=block(src, peer),
            dst_ref=block(dst, me),
            send_sem=send_sem.at[k],
            recv_sem=recv_sem.at[k],
            device_id={"seq": peer},
            device_id_type=MESH,
        )

    def arrival(k):
        holder = lax.rem(me + n - k, n)
        return pltpu.make_async_remote_copy(
            src_ref=block(src, holder),
            dst_ref=block(dst, holder),
            send_sem=send_sem.at[k],
            recv_sem=recv_sem.at[k],
            device_id={"seq": holder},
            device_id_type=MESH,
        )

    def start(i, carry):
        remote(i + 1).start()
        return carry

    def received(k, carry):
        arrival(k).wait_recv()
        return carry

    def sent(k, carry):
        remote(k).wait_send()
        return carry

    def start_all():
        own.start()
        lax.fori_loop(0, n - 1, start, 0)

    def wait_received():
        own.wait()
        lax.fori_loop(1, n, received, 0)

    def wait_sent():
        lax.fori_loop(1, n, sent, 0)

    return start_all, wait_received, wait_sent


def kernel(
    n, spans, length, plan_ref, enc_ref, q_hbm, g_hbm, wk_hbm, wv_hbm,
    qg_hbm, grad_ref,
    want, asked, outgoing, arr, q, g, wk, wv, qg, key_sum, val_sum, keys, vals, kg, vg, ret, came,
    sem, wsem, own, ids_s, ids_r, out_s, out_r, back_s, back_r,
):
    me = lax.axis_index("seq")
    parts = own.shape[1]
    wide = enc_ref.shape[1] // parts
    width = 256
    head = D // HEADS
    span = q.shape[0] // spans
    pair = keys.shape[0] // spans
    size = want.shape[0] // n
    count, slots, held = keys.shape[0], arr.shape[0], enc_ref.shape[0]
    scaling = 1.0 / math.sqrt(head)

    weights = []
    for j in range(parts):
        rows = pl.ds(j * wide, wide)
        both = [
            pltpu.make_async_copy(h.at[rows], v.at[rows], wsem.at[i, j])
            for i, (h, v) in enumerate(((wk_hbm, wk), (wv_hbm, wv)))
        ]
        for copy in both:
            copy.start()
        weights.append(both)
    loads = [
        pltpu.make_async_copy(q_hbm, q, sem.at[0]),
        pltpu.make_async_copy(g_hbm, g, sem.at[1]),
    ]
    for copy in loads:
        copy.start()

    def down(line, rows, each):
        shape = (rows, line.shape[1])
        here = lax.broadcasted_iota(jnp.int32, shape, 0) // each
        here = here == lax.broadcasted_iota(jnp.int32, shape, 1)
        picked_out = jnp.sum(jnp.where(here, line, 0.0), axis=1, keepdims=True)
        return picked_out.astype(jnp.int32)

    places = plan_ref[0:1, :].astype(F32)
    token = lax.rem(lax.broadcasted_iota(jnp.int32, (slots, 1), 0), length)
    row = down(plan_ref[1:2, :].astype(F32), slots, length)
    row = jnp.where(row >= 0, row * length + token, -1)
    want[...] = jnp.broadcast_to(row, want.shape)

    greet(n, me)
    start, received, sent = exchange(
        n, me, size, want, asked, slice(None), ids_s, ids_r, sem.at[2]
    )
    start()
    received()
    sent()
    select = one_hot(asked[:, 0:1], (slots, held), 1)

    def fetch(j):
        return exchange(
            n, me, size, outgoing, arr, tile(j, wide), out_s.at[j], out_r.at[j], own.at[0, j]
        )

    def serve(j, carry):
        cols = tile(j, wide)
        outgoing[:, cols] = jnp.dot(
            select, enc_ref[:, cols], preferred_element_type=F32
        ).astype(BF16)
        fetch(j)[0]()
        return carry

    lax.fori_loop(0, parts, serve, 0)

    place = down(places, count, length) * length + token[:count]
    gather = one_hot(place, (count, slots), 1)
    for j in range(parts):
        for copy in weights[j]:
            copy.wait()
        fetch(j)[1]()
        deep = slice(j * wide, (j + 1) * wide)
        picked = jnp.dot(gather, arr[:, deep], preferred_element_type=F32).astype(BF16)

        def project(i, carry):
            cols = tile(i, width)
            for w, total, result in ((wk, key_sum, keys), (wv, val_sum, vals)):
                part = jnp.dot(picked, w[deep, cols], preferred_element_type=F32)
                if j > 0:
                    part = part + total[:, cols]
                if j < parts - 1:
                    total[:, cols] = part
                else:
                    result[:, cols] = part.astype(BF16)
            return carry

        lax.fori_loop(0, D // width, project, 0)
    for copy in loads:
        copy.wait()

    def attend(c, together):
        toks = pl.ds(pl.multiple_of(c * span, span), together * span)
        nbrs = pl.ds(pl.multiple_of(c * pair, pair), together * pair)
        rows, lanes = 2 * together * pair, together * span
        own = lax.rem(lax.broadcasted_iota(jnp.int32, (rows, lanes), 0) // pair, together)
        mine = own == lax.broadcasted_iota(jnp.int32, (rows, lanes), 1) // span
        gap = jnp.zeros((together * pair, head), BF16)

        def apart(two):
            upper = jnp.concatenate([two[:, :head], gap], axis=1)
            return jnp.concatenate([upper, jnp.concatenate([gap, two[:, head:]], axis=1)], axis=0)

        for h in range(0, HEADS, 2):
            cols = slice(h * head, (h + 2) * head)
            one, two = slice(h * head, (h + 1) * head), slice((h + 1) * head, (h + 2) * head)
            half = together * pair
            qh, gh = q[toks, cols], g[toks, cols]
            kh, vh = apart(keys[nbrs, cols]), apart(vals[nbrs, cols])
            scores = lax.dot_general(kh, qh, NT, preferred_element_type=F32) * scaling
            scores = jnp.where(mine, scores, -jnp.inf).reshape(2, half, lanes)
            raised = jnp.exp(scores - jnp.max(scores, axis=1, keepdims=True))
            probs = raised * (1.0 / jnp.sum(raised, axis=1, keepdims=True))
            probs_b = probs.astype(BF16)
            dprobs = lax.dot_general(vh, gh, NT, preferred_element_type=F32)
            dprobs = dprobs.reshape(2, half, lanes)
            delta = jnp.sum(probs_b.astype(F32) * dprobs, axis=1, keepdims=True)
            dscores = (probs * (dprobs - delta)).astype(BF16).reshape(rows, lanes)
            dq = lax.dot_general(dscores, kh, TN, preferred_element_type=F32) * scaling
            qg[toks, cols] = dq.astype(BF16)
            dk = jnp.dot(dscores, qh, preferred_element_type=F32)
            kg[nbrs, one] = (dk[:half, :head] * scaling).astype(BF16)
            kg[nbrs, two] = (dk[half:, head:] * scaling).astype(BF16)
            dv = jnp.dot(probs_b.reshape(rows, lanes), gh, preferred_element_type=F32)
            vg[nbrs, one] = dv[:half, :head].astype(BF16)
            vg[nbrs, two] = dv[half:, head:].astype(BF16)

    def attend_two(i, carry):
        attend(i * 2, 2)
        return carry

    lax.fori_loop(0, spans // 2, attend_two, 0)
    if spans % 2:
        attend(spans - 1, 1)
    query_done = pltpu.make_async_copy(qg, qg_hbm, sem.at[3])
    query_done.start()
    refs = count // length
    level = lax.broadcasted_iota(jnp.int32, (refs, count), 1)
    here = lax.broadcasted_iota(jnp.int32, (refs, count), 0) == level // length
    across = jnp.where(here, down(places, refs, 1), 0)
    across = jnp.sum(across.astype(F32), axis=0, keepdims=True).astype(jnp.int32)
    across = across * length + lax.rem(level[0:1, :], length)
    spread = one_hot(across, (slots, count), 0)

    def give_back(j):
        return exchange(
            n, me, size, ret, came, tile(j, wide), back_s.at[j], back_r.at[j], own.at[1, j]
        )

    def back(j, carry):
        cols = tile(j, wide)
        total = lax.dot_general(kg[...], wk[cols, :], NT, preferred_element_type=F32)
        total = total + lax.dot_general(vg[...], wv[cols, :], NT, preferred_element_type=F32)
        ret[:, cols] = jnp.dot(
            spread, total.astype(BF16), preferred_element_type=F32
        ).astype(BF16)
        give_back(j)[0]()
        return carry

    lax.fori_loop(0, parts, back, 0)

    def finish(j, carry):
        give_back(j)[1]()
        cols = tile(j, wide)
        grad_ref[:, cols] = lax.dot_general(
            select, came[:, cols], TN, preferred_element_type=F32
        ).astype(BF16)
        fetch(j)[2]()
        give_back(j)[2]()
        return carry

    lax.fori_loop(0, parts, finish, 0)
    query_done.wait()


def on_device_whole_heads(queries, out_grad, encodings, key_weight, value_weight, neighbours):
    n = lax.axis_size("seq")
    spans = neighbours.shape[0]
    refs = 2 * spans
    rows, length, width = encodings.shape
    toks = queries.shape[0]
    capacity = max(2, refs // n)
    slots = n * capacity
    ids = neighbours.reshape(refs)
    owner = ids // rows
    place = owner * capacity + slot_ranks(owner)
    hit = place[None, :] == jnp.arange(slots, dtype=jnp.int32)[:, None]
    row = jnp.max(jnp.where(hit, (ids % rows)[None, :], -1), axis=1)
    lanes = -(-max(slots, refs) // 128) * 128
    plan = jnp.stack([jnp.pad(place, (0, lanes - refs)), jnp.pad(row, (0, lanes - slots))])
    vmem = pl.BlockSpec(memory_space=pltpu.VMEM)
    hbm = pl.BlockSpec(memory_space=pl.ANY)
    dma = pltpu.SemaphoreType.DMA
    total = slots * length
    count = refs * length
    parts = 4
    query_grad, encoding_grad = pl.pallas_call(
        functools.partial(kernel, n, spans, length),
        out_shape=(
            jax.ShapeDtypeStruct((toks, width), BF16),
            jax.ShapeDtypeStruct((rows * length, width), BF16),
        ),
        in_specs=[vmem, vmem, hbm, hbm, hbm, hbm],
        out_specs=(hbm, vmem),
        scratch_shapes=[
            pltpu.VMEM((total, 128), jnp.int32),
            pltpu.VMEM((total, 128), jnp.int32),
            pltpu.VMEM((total, width), BF16),
            pltpu.VMEM((total, width), BF16),
            pltpu.VMEM((toks, width), BF16),
            pltpu.VMEM((toks, width), BF16),
            pltpu.VMEM((width, width), BF16),
            pltpu.VMEM((width, width), BF16),
            pltpu.VMEM((toks, width), BF16),
            pltpu.VMEM((count, width), F32),
            pltpu.VMEM((count, width), F32),
            pltpu.VMEM((count, width), BF16),
            pltpu.VMEM((count, width), BF16),
            pltpu.VMEM((count, width), BF16),
            pltpu.VMEM((count, width), BF16),
            pltpu.VMEM((total, width), BF16),
            pltpu.VMEM((total, width), BF16),
            dma((4,)), dma((2, parts)), dma((2, parts)),
            dma((n,)), dma((n,)),
            dma((parts, n)), dma((parts, n)), dma((parts, n)), dma((parts, n)),
        ],
        compiler_params=pltpu.CompilerParams(
            collective_id=0, has_side_effects=True, vmem_limit_bytes=58 << 20
        ),
    )(
        plan, encodings.reshape(rows * length, width),
        queries, out_grad, key_weight, value_weight,
    )
    return query_grad, encoding_grad.reshape(rows, length, width)


def slot_ranks(owner_ids):
    count = owner_ids.shape[-1]
    same_owner = owner_ids[..., :, None] == owner_ids[..., None, :]
    positions = jnp.arange(count, dtype=jnp.int32)
    earlier = positions[None, :] < positions[:, None]
    return jnp.sum(same_owner & earlier, axis=-1)


def on_device(queries, out_grad, encodings, key_weight, value_weight, neighbours):
    seq_count = lax.axis_size("seq")
    seq_index = lax.axis_index("seq")
    spans_here = neighbours.shape[0]
    ref_count = 2 * spans_here
    rows_here, neighbour_len, half_width = encodings.shape
    full_width = key_weight.shape[0]
    tok_rows = queries.shape[0]
    span_len = tok_rows // spans_here
    head_size = D // HEADS
    heads_here = half_width // head_size
    scaling = 1.0 / math.sqrt(head_size)
    capacity = max(2, ref_count // seq_count)
    slot_count = seq_count * capacity
    all_lists = lax.all_gather(neighbours, "seq", axis=0, tiled=True).reshape(seq_count, ref_count)
    owner_table = all_lists // rows_here
    local_table = all_lists % rows_here
    rank_table = slot_ranks(owner_table)
    own_ids = neighbours.reshape(ref_count)
    own_owner = own_ids // rows_here
    position = own_owner * capacity + slot_ranks(own_owner)
    slot_ids = jnp.arange(capacity, dtype=jnp.int32)
    chosen = (owner_table == seq_index)[:, None, :] & (
        rank_table[:, None, :] == slot_ids[None, :, None]
    )
    filled = jnp.any(chosen, axis=-1)
    slot_row = jnp.sum(jnp.where(chosen, local_table[:, None, :], 0), axis=-1)
    select = filled[..., None] & (
        slot_row[..., None] == jnp.arange(rows_here, dtype=jnp.int32)[None, None, :]
    )
    select = select.astype(jnp.bfloat16).reshape(slot_count, rows_here)
    flat_enc = encodings.reshape(rows_here, neighbour_len * half_width)
    outgoing = jnp.dot(select, flat_enc, preferred_element_type=jnp.float32).astype(jnp.bfloat16)
    outgoing = outgoing.reshape(seq_count, capacity, neighbour_len, half_width)
    arrived = lax.all_to_all(outgoing, "seq", split_axis=0, concat_axis=0, tiled=True)
    flat_arrived = arrived.reshape(slot_count, neighbour_len, half_width)
    whole = lax.all_gather(flat_arrived, "head", axis=2, tiled=True)
    pick = (position[:, None] == jnp.arange(slot_count, dtype=jnp.int32)[None, :]).astype(
        jnp.bfloat16
    )
    full_rows = jnp.dot(
        pick, whole.reshape(slot_count, neighbour_len * full_width),
        preferred_element_type=jnp.float32,
    ).astype(jnp.bfloat16)
    flat_rows = full_rows.reshape(ref_count * neighbour_len, full_width)
    keys = jnp.dot(flat_rows, key_weight, preferred_element_type=jnp.float32).astype(jnp.bfloat16)
    values = jnp.dot(flat_rows, value_weight, preferred_element_type=jnp.float32).astype(
        jnp.bfloat16
    )
    query_heads = queries.reshape(spans_here, span_len, heads_here, head_size)
    grad_heads = out_grad.reshape(spans_here, span_len, heads_here, head_size)
    key_heads = keys.reshape(spans_here, 2 * neighbour_len, heads_here, head_size)
    value_heads = values.reshape(spans_here, 2 * neighbour_len, heads_here, head_size)
    scores = (
        jnp.einsum("cthd,cuhd->chtu", query_heads, key_heads, preferred_element_type=jnp.float32)
        * scaling
    )
    scores = scores - jnp.max(scores, axis=-1, keepdims=True)
    raised = jnp.exp(scores)
    probs = raised / jnp.sum(raised, axis=-1, keepdims=True)
    probs_b = probs.astype(jnp.bfloat16)
    attended = jnp.einsum(
        "chtu,cuhd->cthd", probs_b, value_heads, preferred_element_type=jnp.float32
    )
    delta = jnp.transpose(jnp.sum(grad_heads.astype(jnp.float32) * attended, axis=-1), (0, 2, 1))
    dprobs = jnp.einsum(
        "cthd,cuhd->chtu", grad_heads, value_heads, preferred_element_type=jnp.float32
    )
    dscores = (probs * (dprobs - delta[..., None])).astype(jnp.bfloat16)
    query_grad = (
        jnp.einsum("chtu,cuhd->cthd", dscores, key_heads, preferred_element_type=jnp.float32)
        * scaling
    )
    query_grad = query_grad.astype(jnp.bfloat16).reshape(tok_rows, half_width)
    key_grad = (
        jnp.einsum("chtu,cthd->cuhd", dscores, query_heads, preferred_element_type=jnp.float32)
        * scaling
    )
    key_grad = key_grad.astype(jnp.bfloat16).reshape(ref_count * neighbour_len, half_width)
    value_grad = jnp.einsum(
        "chtu,cthd->cuhd", probs_b, grad_heads, preferred_element_type=jnp.float32
    )
    value_grad = value_grad.astype(jnp.bfloat16).reshape(ref_count * neighbour_len, half_width)
    contract = (((1,), (1,)), ((), ()))
    partial_value = lax.dot_general(
        key_grad, key_weight, contract, preferred_element_type=jnp.float32
    )
    partial_value = partial_value + lax.dot_general(
        value_grad, value_weight, contract, preferred_element_type=jnp.float32
    )
    summed = lax.psum_scatter(
        partial_value.reshape(ref_count, neighbour_len, full_width),
        "head",
        scatter_dimension=2,
        tiled=True,
    )
    ref_grad = summed.astype(jnp.bfloat16)
    returning = (
        jnp.zeros((slot_count, neighbour_len, half_width), jnp.bfloat16).at[position].set(ref_grad)
    )
    returning = returning.reshape(seq_count, capacity, neighbour_len, half_width)
    came_back = lax.all_to_all(returning, "seq", split_axis=0, concat_axis=0, tiled=True).reshape(
        slot_count, neighbour_len * half_width
    )
    encoding_grad = lax.dot_general(
        select, came_back, (((0,), (0,)), ((), ())), preferred_element_type=jnp.float32
    )
    encoding_grad = encoding_grad.astype(jnp.bfloat16).reshape(rows_here, neighbour_len, half_width)
    return (query_grad, encoding_grad)


def solution(mesh):
    body = on_device_whole_heads if mesh.shape["head"] == 1 else on_device
    return jax.shard_map(
        body,
        mesh=mesh,
        in_specs=(
            P(("dp", "seq"), "head"),
            P(("dp", "seq"), "head"),
            P(("dp", "seq"), None, "head"),
            P(None, "head"),
            P(None, "head"),
            P(("dp", "seq"), None),
        ),
        out_specs=(P(("dp", "seq"), "head"), P(("dp", "seq"), None, "head")),
        check_vma=False,
    )
```
